32 devices in a mesh: grp: 4 (over y, x), dev: 8 (over z, core).
Axes of the slice: x: 2, y: 2, z: 4, core: 2. Of those that a mesh axis runs over, the one named last changes fastest.
Arguments:
- adjacency: float32 [256, 1024, 128], P('dev', 'grp'), may hold values from 0.05 to 5
- features: float32 [32768, 256], P('dev', 'grp'), may hold values from -6 to 6
- col_slot: int32 [256, 128], P('dev'), may hold values from 0 to 127, each once within a row
- row_slot: int32 [8, 128], P('grp'), may hold values from 0 to 127, each once within a row
- row_pair: int32 [8], replicated, may hold values from 0 to 7, each once
- col_pair: int32 [32], replicated, may hold values from 0 to 31, each once
- col_offset: int32 [32], replicated, may hold values from 0 to 7, as said below
Outputs:
- coarse_adjacency: float32 [128, 512, 128], P('dev', 'grp')
- coarse_features: float32 [16384, 256], P('dev', 'grp')
The draws below stay inside these ranges and needn't reach their ends.
Inputs may be any that keep to these rules, and one draw needn't show every extreme that they name: `col_offset`: each value appears at most 8 times; some value appears exactly 8 times.
All inputs are finite; a program needn't handle non-finite values.
Results may differ from the reference program's by a relative error of at most 0.00007.
Values sent between devices are 32-bit elements; how exact they have to be, the bound alone decides.
No kernel may reach another device: no remote copies, remote signals or barrier semaphores. Data moves between devices by JAX's collectives and lax.ppermute only.
A program may use at most 64 MiB of HBM per device.

```python
import math
import jax
import jax.numpy as jnp

TILE = 128
FEAT = 256
CBD = 32
NB = 256
NR = 8
NC = 128
NRC = 4
NCD = 16
N_DEV = 8


def draw_col_offset(key, part):
    key = jax.random.fold_in(key, 7)
    key_count, key_values, key_order = jax.random.split(key, 3)
    per_value = CBD // N_DEV
    most_doubled = min(16, N_DEV // 2)
    doubled = jax.random.randint(key_count, (), 2, most_doubled + 1)
    ranking = jax.random.permutation(key_values, N_DEV).astype(jnp.int32)
    by_rank = jnp.zeros((N_DEV,), jnp.int32).at[ranking].set(jnp.arange(N_DEV, dtype=jnp.int32))
    residues = jnp.arange(CBD, dtype=jnp.int32) // per_value
    standing = ranking[residues]
    emptied = jnp.logical_and(standing >= doubled, standing < 2 * doubled)
    partner = by_rank[jnp.clip(standing - doubled, 0, N_DEV - 1)]
    residues = jnp.where(emptied, partner, residues)
    return jax.random.permutation(key_order, residues).astype(jnp.int32)


def shard_levels(key, dims, cuts, least, top_value):
    def one(dim, blocks):
        heights = jax.random.uniform(jax.random.fold_in(jax.random.fold_in(key, 6), dim), (blocks,), jnp.float32, least / len(cuts), top_value / len(cuts))
        return jnp.repeat(jnp.exp(heights), dims[dim] // blocks).reshape((-1,) + (1,) * (len(dims) - dim - 1))

    factor_of = one(*cuts[0])
    for cut in cuts[1:]:
        factor_of = factor_of * one(*cut)
    return factor_of


def gaussian(own_key, extent, spread, limit, cuts=(), kind=jnp.bfloat16):
    array = jax.random.normal(own_key, extent, jnp.float32) * spread
    if len(cuts) > 0:
        array = shard_levels(own_key, extent, cuts, -0.22, 0.18) * array
    return jnp.clip(array, min=-limit, max=limit).astype(kind)


def setup_inputs(seed: int = 0) -> dict:
    splits = jax.random.split(jax.random.key(seed), 8)
    adjacency = jnp.clip(jnp.exp(math.log(5.0) - 4.6051702 * jax.random.uniform(splits[0], (NB, NR * TILE, TILE), jnp.float32) ** shard_levels(splits[0], (NB, NR * TILE, TILE), ((0, 8), (1, 4)), -0.2, 0.2)), 0.05, 5.0)
    features = gaussian(splits[1], (NB * TILE, FEAT), 1.0, 6.0, ((0, 8), (1, 4)), jnp.float32)
    col_slot = jax.vmap(lambda own: jax.random.permutation(own, TILE))(jax.random.split(splits[2], NB)).reshape((NB, TILE)).astype(jnp.int32)
    row_slot = jax.vmap(lambda own: jax.random.permutation(own, TILE))(jax.random.split(splits[3], NR)).reshape((NR, TILE)).astype(jnp.int32)
    row_pair = jax.random.permutation(splits[4], NR).astype(jnp.int32)
    col_pair = jax.random.permutation(splits[5], CBD).astype(jnp.int32)
    col_offset = draw_col_offset(jax.random.fold_in(splits[7], 71), 0)
    return dict(adjacency=adjacency, features=features, col_slot=col_slot, row_slot=row_slot, row_pair=row_pair, col_pair=col_pair, col_offset=col_offset)


def reference(adjacency, features, col_slot, row_slot, row_pair, col_pair, col_offset):
    inverse = jnp.argsort(col_slot, axis=1).astype(jnp.int32)
    permuted = jnp.take_along_axis(adjacency, inverse[:, None, :], axis=2)
    row_place = jnp.argsort(row_pair).astype(jnp.int32)
    coarse_row = row_place // 2
    target = (coarse_row[:, None] * TILE + row_slot).reshape(-1)
    row_sums = jnp.zeros((NB, NRC * TILE, TILE), adjacency.dtype).at[:, target].add(permuted)
    block_ids = jnp.arange(NB, dtype=jnp.int32)
    position = block_ids % CBD
    owner_dev = (block_ids // CBD + col_offset[position]) % N_DEV
    col_place = jnp.argsort(col_pair).astype(jnp.int32)
    coarse_id = owner_dev * NCD + col_place[position] // 2
    coarse_adjacency = jnp.zeros((NC, NRC * TILE, TILE), adjacency.dtype).at[coarse_id].add(row_sums)
    feat_blocks = features.reshape(NB, TILE, FEAT)
    feat_perm = jnp.take_along_axis(feat_blocks, inverse[:, :, None], axis=1)
    coarse_feats = jnp.zeros((NC, TILE, FEAT), features.dtype).at[coarse_id].add(feat_perm)
    return coarse_adjacency, coarse_feats.reshape(NC * TILE, FEAT)
```

```python
import functools
import jax
import jax.numpy as jnp
from jax import lax
from jax.experimental import pallas as pl
from jax.experimental.pallas import tpu as pltpu
from jax.sharding import PartitionSpec as P

TILE = 128
GROUPS = 4
ANY = pl.BlockSpec(memory_space=pl.ANY)
VMEM = pl.BlockSpec(memory_space=pltpu.VMEM)
SMEM = pl.BlockSpec(memory_space=pltpu.SMEM)


def split16(x):
    high = x.astype(jnp.bfloat16)
    low = (x - high.astype(jnp.float32)).astype(jnp.bfloat16)
    return high, low


def rows_kernel(first, rows, step_blocks, pair_ref, slot_ref, *refs):
    tiles = refs[: 2 * step_blocks]
    send_x, keep_x, send_y, keep_y, onehot = refs[2 * step_blocks :]

    @pl.when(pl.program_id(0) == 0)
    def _():
        group = lax.axis_index("grp")
        keys = []
        for r in range(2):
            owner = jnp.int32(0)
            for h in range(2 * GROUPS):
                owner = jnp.where(pair_ref[h] == 2 * group + r, h // 2, owner)
            away = jnp.bitwise_xor(owner, group)
            local = slot_ref[r : r + 1, :] - first
            inside = jnp.logical_and(local >= 0, local < rows)
            keys.append(jnp.where(inside, away * rows + local, -1))
        key = jnp.concatenate(keys + keys, axis=1)
        place = lax.broadcasted_iota(jnp.int32, (GROUPS * rows, 4 * TILE), 0)
        onehot[...] = (place == key).astype(jnp.float32).astype(jnp.bfloat16)

    def mapped(pair):
        x = jnp.concatenate([tile[0] for tile in pair], axis=1)
        high, low = split16(x)
        both = jnp.concatenate([high, low], axis=0)
        return jnp.dot(onehot[...], both, preferred_element_type=jnp.float32)

    for i in range(0, step_blocks, 2):
        full = mapped(tiles[i : i + 2])
        for j in range(2):
            lanes = slice(j * TILE, (j + 1) * TILE)
            part = [full[m * rows : (m + 1) * rows, lanes] for m in range(GROUPS)]
            keep_x[0, i + j], send_x[0, i + j], keep_x[1, i + j], send_x[1, i + j] = part
        full = mapped(tiles[step_blocks + i : step_blocks + i + 2])
        for j in range(2):
            lanes = slice(j * TILE, (j + 1) * TILE)
            part = [full[m * rows : (m + 1) * rows, lanes] for m in range(GROUPS)]
            keep_y[0, i + j], keep_y[1, i + j], send_y[0, i + j], send_y[1, i + j] = part


def row_map(adjacency, row_slot, row_pair, first, rows):
    blocks, own_rows, tile = adjacency.shape
    half = blocks // 2
    step_blocks = 4
    steps = half // step_blocks

    def at(base, j):
        return pl.BlockSpec((1, own_rows, tile), lambda i: (base + step_blocks * i + j, 0, 0))

    out = jax.ShapeDtypeStruct((2, half, rows, tile), jnp.float32)
    return pl.pallas_call(
        functools.partial(rows_kernel, first, rows, step_blocks),
        grid=(steps,),
        out_shape=[out] * 4,
        in_specs=[SMEM, VMEM]
        + [at(0, j) for j in range(step_blocks)]
        + [at(half, j) for j in range(step_blocks)],
        out_specs=[pl.BlockSpec((2, step_blocks, rows, tile), lambda i: (0, i, 0, 0))] * 4,
        scratch_shapes=[pltpu.VMEM((GROUPS * rows, 4 * tile), jnp.bfloat16)],
        compiler_params=pltpu.CompilerParams(vmem_limit_bytes=32 << 20),
        cost_estimate=pl.CostEstimate(flops=int(2e9), bytes_accessed=12 << 20, transcendentals=0),
        name="row_map",
    )(row_pair, row_slot, *([adjacency] * (2 * step_blocks)))


def lanes_of(x, slots):
    place = lax.broadcasted_iota(jnp.int32, (TILE, TILE), 0)
    onehot = (place == slots).astype(jnp.float32).astype(jnp.bfloat16)
    high, low = split16(x)
    both = lax.dot_general(
        jnp.concatenate([high, low], axis=0),
        onehot,
        (((1,), (1,)), ((), ())),
        preferred_element_type=jnp.float32,
    )
    return both[: x.shape[0]] + both[x.shape[0] :]


def features_kernel(blocks, slot_ref, col_ref, x_ref, out_ref):
    for p in range(blocks):
        lanes = slice(p * TILE, (p + 1) * TILE)
        out_ref[slot_ref[p]] = lanes_of(x_ref[:, lanes], col_ref[p : p + 1, :])
    for p in range(blocks, out_ref.shape[0]):
        out_ref[p] = jnp.zeros(out_ref.shape[1:], jnp.float32)


def columns_kernel(step_blocks, steps, slot_ref, col_ref, *refs):
    ins, out_ref = refs[:6], refs[6]
    i = pl.program_id(0)
    for half in range(2):
        keep, got1, got2 = ins[3 * half : 3 * half + 3]
        for j in range(step_blocks):
            p = half * steps * step_blocks + i * step_blocks + j
            x = keep[0, j] + got1[0, j] + got2[j]
            out_ref[slot_ref[p]] = lanes_of(x, col_ref[pl.ds(p, 1), :])

    @pl.when(i == 0)
    def _():
        for p in range(2 * steps * step_blocks, out_ref.shape[0]):
            out_ref[p] = jnp.zeros(out_ref.shape[1:], jnp.float32)


def column_map(keep_x, got1_x, got2_x, keep_y, got1_y, got2_y, col_slot, slot, pad):
    half, rows, tile = got2_x.shape
    step_blocks = 4
    steps = half // step_blocks
    four = pl.BlockSpec((1, step_blocks, rows, tile), lambda i: (0, i, 0, 0))
    three = pl.BlockSpec((step_blocks, rows, tile), lambda i: (i, 0, 0))
    shape = (2 * half + pad, rows, tile)
    return pl.pallas_call(
        functools.partial(columns_kernel, step_blocks, steps),
        grid=(steps,),
        out_shape=jax.ShapeDtypeStruct(shape, jnp.float32),
        in_specs=[SMEM, VMEM] + [four, four, three] * 2,
        out_specs=pl.BlockSpec(shape, lambda i: (0, 0, 0)),
        compiler_params=pltpu.CompilerParams(vmem_limit_bytes=32 << 20),
        cost_estimate=pl.CostEstimate(flops=int(1e9), bytes_accessed=4 << 20, transcendentals=0),
        name="column_map",
    )(slot, col_slot, keep_x, got1_x, got2_x, keep_y, got1_y, got2_y)


def feature_map(features_t, col_slot, slot, pad):
    width, columns = features_t.shape
    blocks = columns // TILE
    return pl.pallas_call(
        functools.partial(features_kernel, blocks),
        out_shape=jax.ShapeDtypeStruct((blocks + pad, width, TILE), jnp.float32),
        in_specs=[SMEM, VMEM, VMEM],
        out_specs=VMEM,
        compiler_params=pltpu.CompilerParams(vmem_limit_bytes=32 << 20),
        cost_estimate=pl.CostEstimate(flops=int(1e9), bytes_accessed=2 << 20, transcendentals=0),
        name="feature_map",
    )(slot, col_slot, features_t)


def merge_kernel(sizes, in_lanes, src_ref, *refs):
    pieces = refs[: len(sizes)]
    out_ref, held, sem = refs[-3:]
    copies = []
    at = 0
    for n, (piece, size) in enumerate(zip(pieces, sizes)):
        copies.append(
            pltpu.make_async_copy(piece.at[pl.ds(0, size)], held.at[pl.ds(at, size)], sem.at[n])
        )
        at += size
    for copy in copies:
        copy.start()
    for copy in copies:
        copy.wait()
    count = src_ref.shape[0] // 2
    for k in range(count):
        total = held[src_ref[2 * k]] + held[src_ref[2 * k + 1]]
        if in_lanes:
            out_ref[:, k * TILE : (k + 1) * TILE] = total
        else:
            out_ref[k] = total


def merge_features(pieces, sizes, src):
    width = pieces[0].shape[1]
    count = src.shape[0] // 2
    return pl.pallas_call(
        functools.partial(merge_kernel, sizes, True),
        out_shape=jax.ShapeDtypeStruct((width, count * TILE), jnp.float32),
        in_specs=[SMEM] + [ANY] * len(pieces),
        out_specs=VMEM,
        scratch_shapes=[
            pltpu.VMEM((sum(sizes), width, TILE), jnp.float32),
            pltpu.SemaphoreType.DMA((len(pieces),)),
        ],
        compiler_params=pltpu.CompilerParams(vmem_limit_bytes=32 << 20),
        cost_estimate=pl.CostEstimate(flops=int(1e6), bytes_accessed=3 << 20, transcendentals=0),
        name="merge_features",
    )(src, *pieces)


def merge_tiles(pieces, sizes, src, first, before):
    rows = pieces[0].shape[1]
    count = src.shape[0] // 2
    operands = (src, *pieces) + (() if before is None else (before,))
    return pl.pallas_call(
        functools.partial(merge_kernel, sizes, False),
        grid=(1,),
        out_shape=jax.ShapeDtypeStruct((count, TILE, TILE), jnp.float32),
        in_specs=[SMEM] + [ANY] * (len(operands) - 1),
        out_specs=pl.BlockSpec((count, rows, TILE), lambda i: (0, first // rows, 0)),
        input_output_aliases={} if before is None else {len(operands) - 1: 0},
        scratch_shapes=[
            pltpu.VMEM((sum(sizes), rows, TILE), jnp.float32),
            pltpu.SemaphoreType.DMA((len(pieces),)),
        ],
        compiler_params=pltpu.CompilerParams(vmem_limit_bytes=32 << 20),
        cost_estimate=pl.CostEstimate(flops=int(1e6), bytes_accessed=3 << 20, transcendentals=0),
        name="merge_tiles",
    )(*operands)


def turn(x, shift, dev_count):
    return lax.ppermute(x, "dev", [(i, (i + shift) % dev_count) for i in range(dev_count)])


def exchange_some(sorted_blocks, counts, starts, capacity, dev_count):
    unit = capacity // 2
    rest = sorted_blocks.shape[1:]

    def branch(shift, units):
        def run(blocks, start):
            if units == 0:
                return jnp.zeros((capacity,) + rest, jnp.float32)
            size = units * unit
            piece = lax.dynamic_slice(blocks, (start, 0, 0), (size,) + rest)
            got = turn(piece, shift, dev_count)
            if size < capacity:
                got = jnp.concatenate([got, jnp.zeros((capacity - size,) + rest, jnp.float32)])
            return got

        return run

    pieces = [sorted_blocks]
    for shift in range(1, dev_count):
        units = (counts[shift] + unit - 1) // unit
        pieces.append(
            lax.switch(units, [branch(shift, u) for u in range(3)], sorted_blocks, starts[shift])
        )
    return pieces, [capacity] * dev_count


def exchange_all(sorted_blocks, counts, starts, capacity, dev_count):
    me = lax.axis_index("dev")
    ids = jnp.arange(dev_count * capacity, dtype=jnp.int32)
    shift = (ids // capacity - me) % dev_count
    send = jnp.take(sorted_blocks, jnp.take(starts, shift) + ids % capacity, axis=0)
    got = lax.all_to_all(send, "dev", split_axis=0, concat_axis=0, tiled=True)
    source = (me - ids // capacity) % dev_count
    return [jnp.take(got, source * capacity + ids % capacity, axis=0)], [dev_count * capacity]


def body(adjacency, features, col_slot, row_slot, row_pair, col_pair, col_offset):
    dev_count = lax.axis_size("dev")
    blocks = adjacency.shape[0]
    half = blocks // 2
    capacity = 2 * blocks // dev_count
    exchange = exchange_some if dev_count == 8 else exchange_all

    positions = jnp.arange(blocks, dtype=jnp.int32)
    same = col_offset[:, None] == col_offset[None, :]
    earlier = positions[None, :] < positions[:, None]
    rank = jnp.sum(jnp.logical_and(same, earlier).astype(jnp.int32), axis=1)
    lower = (col_offset[None, :] < col_offset[:, None]).astype(jnp.int32)
    slot = rank + jnp.sum(lower, axis=1)
    offsets = jnp.arange(dev_count, dtype=jnp.int32)
    counts = jnp.sum((col_offset[None, :] == offsets[:, None]).astype(jnp.int32), axis=1)
    starts = jnp.sum((col_offset[None, :] < offsets[:, None]).astype(jnp.int32), axis=1)
    chosen = col_pair[:, None] == positions[None, :]
    src = jnp.sum(jnp.where(chosen, (col_offset * capacity + rank)[None, :], 0), axis=1)

    x_side = [(g, g ^ 1) for g in range(GROUPS)]
    y_side = [(g, g ^ 2) for g in range(GROUPS)]

    feature_blocks = feature_map(features.T, col_slot, slot, capacity)
    pieces, sizes = exchange(feature_blocks, counts, starts, capacity, dev_count)
    coarse_features = merge_features(pieces, sizes, src).T

    coarse_adjacency = None
    rows = TILE // 2
    for first in range(0, TILE, rows):
        send_x, keep_x, send_y, keep_y = row_map(adjacency, row_slot, row_pair, first, rows)
        got1_x = lax.ppermute(send_x, "grp", x_side)
        got1_y = lax.ppermute(send_y, "grp", y_side)
        got2_x = lax.ppermute(keep_x[1] + got1_x[1], "grp", y_side)
        got2_y = lax.ppermute(keep_y[1] + got1_y[1], "grp", x_side)
        tiles = column_map(
            keep_x, got1_x, got2_x, keep_y, got1_y, got2_y, col_slot, slot, capacity
        )
        pieces, sizes = exchange(tiles, counts, starts, capacity, dev_count)
        coarse_adjacency = merge_tiles(pieces, sizes, src, first, coarse_adjacency)
    return coarse_adjacency, coarse_features


def solution(mesh):
    in_specs = (
        P("dev", "grp", None),
        P("dev", "grp"),
        P("dev", None),
        P("grp", None),
        P(),
        P(),
        P(),
    )
    out_specs = (P("dev", "grp", None), P("dev", "grp"))
    return jax.shard_map(body, mesh=mesh, in_specs=in_specs, out_specs=out_specs, check_vma=False)
```

```python
import functools
import jax
import jax.numpy as jnp
from jax import lax
from jax.experimental import pallas as pl
from jax.experimental.pallas import tpu as pltpu
from jax.sharding import PartitionSpec as P

TILE = 128
GROUPS = 4
ANY = pl.BlockSpec(memory_space=pl.ANY)
VMEM = pl.BlockSpec(memory_space=pltpu.VMEM)
SMEM = pl.BlockSpec(memory_space=pltpu.SMEM)


def split16(x):
    high = x.astype(jnp.bfloat16)
    low = (x - high.astype(jnp.float32)).astype(jnp.bfloat16)
    return high, low


def rows_kernel(first, rows, step_blocks, pair_ref, slot_ref, *refs):
    tiles = refs[: 2 * step_blocks]
    send_x, keep_x, send_y, keep_y, onehot = refs[2 * step_blocks :]

    @pl.when(pl.program_id(0) == 0)
    def _():
        group = lax.axis_index("grp")
        keys = []
        for r in range(2):
            owner = jnp.int32(0)
            for h in range(2 * GROUPS):
                owner = jnp.where(pair_ref[h] == 2 * group + r, h // 2, owner)
            away = jnp.bitwise_xor(owner, group)
            local = slot_ref[r : r + 1, :] - first
            inside = jnp.logical_and(local >= 0, local < rows)
            keys.append(jnp.where(inside, away * rows + local, -1))
        key = jnp.concatenate(keys + keys, axis=1)
        place = lax.broadcasted_iota(jnp.int32, (GROUPS * rows, 4 * TILE), 0)
        onehot[...] = (place == key).astype(jnp.float32).astype(jnp.bfloat16)

    def mapped(pair):
        x = jnp.concatenate([tile[0] for tile in pair], axis=1)
        high, low = split16(x)
        both = jnp.concatenate([high, low], axis=0)
        return jnp.dot(onehot[...], both, preferred_element_type=jnp.float32)

    for i in range(0, step_blocks, 2):
        full = mapped(tiles[i : i + 2])
        for j in range(2):
            lanes = slice(j * TILE, (j + 1) * TILE)
            part = [full[m * rows : (m + 1) * rows, lanes] for m in range(GROUPS)]
            keep_x[0, i + j], send_x[0, i + j], keep_x[1, i + j], send_x[1, i + j] = part
        full = mapped(tiles[step_blocks + i : step_blocks + i + 2])
        for j in range(2):
            lanes = slice(j * TILE, (j + 1) * TILE)
            part = [full[m * rows : (m + 1) * rows, lanes] for m in range(GROUPS)]
            keep_y[0, i + j], keep_y[1, i + j], send_y[0, i + j], send_y[1, i + j] = part


def row_map(adjacency, row_slot, row_pair, first, rows):
    blocks, own_rows, tile = adjacency.shape
    half = blocks // 2
    step_blocks = 4
    steps = half // step_blocks

    def at(base, j):
        return pl.BlockSpec((1, own_rows, tile), lambda i: (base + step_blocks * i + j, 0, 0))

    out = jax.ShapeDtypeStruct((2, half, rows, tile), jnp.float32)
    return pl.pallas_call(
        functools.partial(rows_kernel, first, rows, step_blocks),
        grid=(steps,),
        out_shape=[out] * 4,
        in_specs=[SMEM, VMEM]
        + [at(0, j) for j in range(step_blocks)]
        + [at(half, j) for j in range(step_blocks)],
        out_specs=[pl.BlockSpec((2, step_blocks, rows, tile), lambda i: (0, i, 0, 0))] * 4,
        scratch_shapes=[pltpu.VMEM((GROUPS * rows, 4 * tile), jnp.bfloat16)],
        compiler_params=pltpu.CompilerParams(vmem_limit_bytes=32 << 20),
        cost_estimate=pl.CostEstimate(flops=int(2e9), bytes_accessed=12 << 20, transcendentals=0),
        name="row_map",
    )(row_pair, row_slot, *([adjacency] * (2 * step_blocks)))


def lanes_of(x, slots):
    place = lax.broadcasted_iota(jnp.int32, (TILE, TILE), 0)
    onehot = (place == slots).astype(jnp.float32).astype(jnp.bfloat16)
    high, low = split16(x)
    both = lax.dot_general(
        jnp.concatenate([high, low], axis=0),
        onehot,
        (((1,), (1,)), ((), ())),
        preferred_element_type=jnp.float32,
    )
    return both[: x.shape[0]] + both[x.shape[0] :]


def write_units(held, outs, sem, full):
    copies = []
    for n, out in enumerate(outs):
        size = out.shape[0]
        at = n * size if n < full else (n - full + 1) * 2 * size
        copies.append(pltpu.make_async_copy(held.at[pl.ds(at, size)], out, sem.at[n]))
    for copy in copies:
        copy.start()
    for copy in copies:
        copy.wait()


def features_kernel(blocks, full, slot_ref, col_ref, x_ref, *refs):
    outs, held, sem = refs[:-2], refs[-2], refs[-1]
    for p in range(blocks):
        lanes = slice(p * TILE, (p + 1) * TILE)
        held[slot_ref[p]] = lanes_of(x_ref[:, lanes], col_ref[p : p + 1, :])
    write_units(held, outs, sem, full)


def columns_kernel(step_blocks, steps, full, slot_ref, col_ref, *refs):
    ins, outs, held, sem = refs[:6], refs[6:-2], refs[-2], refs[-1]
    i = pl.program_id(0)
    for half in range(2):
        keep, got1, got2 = ins[3 * half : 3 * half + 3]
        for j in range(step_blocks):
            p = half * steps * step_blocks + i * step_blocks + j
            x = keep[0, j] + got1[0, j] + got2[j]
            held[slot_ref[p]] = lanes_of(x, col_ref[pl.ds(p, 1), :])

    @pl.when(i == steps - 1)
    def _():
        write_units(held, outs, sem, full)


def unit_outputs(full, size, rows):
    half = full - 1
    shapes = [(size, rows, TILE)] * full + [(size // 2, rows, TILE)] * half
    return dict(
        out_shape=[jax.ShapeDtypeStruct(shape, jnp.float32) for shape in shapes],
        out_specs=[ANY] * (full + half),
        scratch_shapes=[
            pltpu.VMEM((full * size, rows, TILE), jnp.float32),
            pltpu.SemaphoreType.DMA((full + half,)),
        ],
    )


def column_map(keep_x, got1_x, got2_x, keep_y, got1_y, got2_y, col_slot, slot, full, size):
    half, rows, tile = got2_x.shape
    step_blocks = 4
    steps = half // step_blocks
    four = pl.BlockSpec((1, step_blocks, rows, tile), lambda i: (0, i, 0, 0))
    three = pl.BlockSpec((step_blocks, rows, tile), lambda i: (i, 0, 0))
    return pl.pallas_call(
        functools.partial(columns_kernel, step_blocks, steps, full),
        grid=(steps,),
        in_specs=[SMEM, VMEM] + [four, four, three] * 2,
        compiler_params=pltpu.CompilerParams(vmem_limit_bytes=32 << 20),
        cost_estimate=pl.CostEstimate(flops=int(1e9), bytes_accessed=4 << 20, transcendentals=0),
        name="column_map",
        **unit_outputs(full, size, rows),
    )(slot, col_slot, keep_x, got1_x, got2_x, keep_y, got1_y, got2_y)


def feature_map(features_t, col_slot, slot, full, size):
    width, columns = features_t.shape
    blocks = columns // TILE
    return pl.pallas_call(
        functools.partial(features_kernel, blocks, full),
        in_specs=[SMEM, VMEM, VMEM],
        compiler_params=pltpu.CompilerParams(vmem_limit_bytes=32 << 20),
        cost_estimate=pl.CostEstimate(flops=int(1e9), bytes_accessed=2 << 20, transcendentals=0),
        name="feature_map",
        **unit_outputs(full, size, width),
    )(slot, col_slot, features_t)


def merge_kernel(count_in, in_lanes, src_ref, *refs):
    pieces = refs[:count_in]
    out_ref, held, sem = refs[-3:]
    copies = []
    at = 0
    for n, piece in enumerate(pieces):
        size = piece.shape[0]
        copies.append(pltpu.make_async_copy(piece, held.at[pl.ds(at, size)], sem.at[n]))
        at += size
    for copy in copies:
        copy.start()
    for copy in copies:
        copy.wait()
    for k in range(src_ref.shape[0] // 2):
        total = held[src_ref[2 * k]] + held[src_ref[2 * k + 1]]
        if in_lanes:
            out_ref[:, k * TILE : (k + 1) * TILE] = total
        else:
            out_ref[k] = total


def merge_scratch(pieces):
    _, rows, tile = pieces[0].shape
    return [
        pltpu.VMEM((sum(piece.shape[0] for piece in pieces), rows, tile), jnp.float32),
        pltpu.SemaphoreType.DMA((len(pieces),)),
    ]


def merge_features(pieces, src):
    width = pieces[0].shape[1]
    count = src.shape[0] // 2
    return pl.pallas_call(
        functools.partial(merge_kernel, len(pieces), True),
        out_shape=jax.ShapeDtypeStruct((width, count * TILE), jnp.float32),
        in_specs=[SMEM] + [ANY] * len(pieces),
        out_specs=VMEM,
        scratch_shapes=merge_scratch(pieces),
        compiler_params=pltpu.CompilerParams(vmem_limit_bytes=32 << 20),
        cost_estimate=pl.CostEstimate(flops=int(1e6), bytes_accessed=3 << 20, transcendentals=0),
        name="merge_features",
    )(src, *pieces)


def merge_tiles(pieces, src, first, before):
    rows = pieces[0].shape[1]
    count = src.shape[0] // 2
    operands = (src, *pieces) + (() if before is None else (before,))
    return pl.pallas_call(
        functools.partial(merge_kernel, len(pieces), False),
        grid=(1,),
        out_shape=jax.ShapeDtypeStruct((count, TILE, TILE), jnp.float32),
        in_specs=[SMEM] + [ANY] * (len(operands) - 1),
        out_specs=pl.BlockSpec((count, rows, TILE), lambda i: (0, first // rows, 0)),
        input_output_aliases={} if before is None else {len(operands) - 1: 0},
        scratch_shapes=merge_scratch(pieces),
        compiler_params=pltpu.CompilerParams(vmem_limit_bytes=32 << 20),
        cost_estimate=pl.CostEstimate(flops=int(1e6), bytes_accessed=3 << 20, transcendentals=0),
        name="merge_tiles",
    )(*operands)


SETS = ((1, 4, 7), (2, 6), (3, 5))


def turn(x, shift, dev_count):
    return lax.ppermute(x, "dev", [(i, (i + shift) % dev_count) for i in range(dev_count)])


def unwritten(shapes):
    return pl.pallas_call(
        lambda *refs: None,
        out_shape=[jax.ShapeDtypeStruct(shape, jnp.float32) for shape in shapes],
        out_specs=[ANY] * len(shapes),
        cost_estimate=pl.CostEstimate(flops=0, bytes_accessed=0, transcendentals=0),
        name="unwritten",
    )()


def exchange_set(which, units, choice, dev_count):
    shifts = SETS[which]
    operands = [units[n] for shift in shifts for n in (shift, dev_count - 1 + shift)]

    def branch(code):
        used = [code // 3**i % 3 for i in range(len(shifts))]
        sent = [(u == 2, u == 1) for u in used]
        sent = [flag for pair in sent for flag in pair]

        def run(*arrays):
            rest = list(unwritten([x.shape for x, flag in zip(arrays, sent) if not flag]))
            got = []
            for n, (array, flag) in enumerate(zip(arrays, sent)):
                got.append(turn(array, shifts[n // 2], dev_count) if flag else rest.pop(0))
            return got

        return run

    return lax.switch(choice[which], [branch(c) for c in range(3 ** len(shifts))], *operands)


def exchange_all(blocks, capacity, dev_count):
    me = lax.axis_index("dev")
    ids = jnp.arange(dev_count * capacity, dtype=jnp.int32)
    away, place = ids // capacity, ids % capacity
    send = jnp.take(blocks, (away - me) % dev_count * capacity + place, axis=0)
    got = lax.all_to_all(send, "dev", split_axis=0, concat_axis=0, tiled=True)
    return jnp.take(got, (me - away) % dev_count * capacity + place, axis=0)


def ordered(first, then):
    first, then = lax.optimization_barrier((first, then))
    return first, then


def body(adjacency, features, col_slot, row_slot, row_pair, col_pair, col_offset):
    dev_count = lax.axis_size("dev")
    blocks = adjacency.shape[0]
    capacity = 2 * blocks // dev_count
    in_sets = dev_count == 8
    full, size = (dev_count, capacity) if in_sets else (1, capacity * dev_count)

    positions = jnp.arange(blocks, dtype=jnp.int32)
    same = col_offset[:, None] == col_offset[None, :]
    earlier = positions[None, :] < positions[:, None]
    rank = jnp.sum(jnp.logical_and(same, earlier).astype(jnp.int32), axis=1)
    slot = col_offset * capacity + rank
    offsets = jnp.arange(dev_count, dtype=jnp.int32)
    counts = jnp.sum((col_offset[None, :] == offsets[:, None]).astype(jnp.int32), axis=1)
    used = (counts > 0).astype(jnp.int32) + (counts > capacity // 2).astype(jnp.int32)
    where = slot
    if in_sets:
        few = jnp.sum(same.astype(jnp.int32), axis=1) <= capacity // 2
        in_half = capacity * dev_count + (col_offset - 1) * (capacity // 2) + rank
        where = jnp.where(jnp.logical_and(few, col_offset > 0), in_half, slot)
    chosen = col_pair[:, None] == positions[None, :]
    src = jnp.sum(jnp.where(chosen, where[None, :], 0), axis=1)

    x_side = [(g, g ^ 1) for g in range(GROUPS)]
    y_side = [(g, g ^ 2) for g in range(GROUPS)]

    def first_step(maps):
        return lax.ppermute(maps[0], "grp", x_side), lax.ppermute(maps[2], "grp", y_side)

    def partial_sums(maps, got):
        return maps[1][1] + got[0][1], maps[3][1] + got[1][1]

    def second_step(sums):
        return lax.ppermute(sums[0], "grp", y_side), lax.ppermute(sums[1], "grp", x_side)

    def columns(maps, got1, got2):
        return column_map(
            maps[1], got1[0], got2[0], maps[3], got1[1], got2[1], col_slot, slot, full, size
        )

    rows = TILE // 2
    maps_a = row_map(adjacency, row_slot, row_pair, 0, rows)
    got1_a = first_step(maps_a)
    maps_a, units_x = ordered(maps_a, feature_map(features.T, col_slot, slot, full, size))

    if not in_sets:
        maps_b = row_map(adjacency, row_slot, row_pair, rows, rows)
        coarse_adjacency = None
        got_x = exchange_all(units_x[0], capacity, dev_count)
        for first, maps in ((0, maps_a), (rows, maps_b)):
            got1 = got1_a if first == 0 else first_step(maps)
            units = columns(maps, got1, second_step(partial_sums(maps, got1)))
            got = exchange_all(units[0], capacity, dev_count)
            coarse_adjacency = merge_tiles([got], src, first, coarse_adjacency)
        return coarse_adjacency, merge_features([got_x], src).T

    weights = [[0] * dev_count for _ in SETS]
    for w, shifts in zip(weights, SETS):
        for i, shift in enumerate(shifts):
            w[shift] = 3**i
    choice = jnp.sum(jnp.array(weights, dtype=jnp.int32) * used[None, :], axis=1)

    def collect(units, parts):
        pieces = list(units)
        for shifts, part in zip(SETS, parts):
            for i, shift in enumerate(shifts):
                pieces[shift], pieces[dev_count - 1 + shift] = part[2 * i], part[2 * i + 1]
        return pieces

    maps_b = row_map(adjacency, row_slot, row_pair, rows, rows)
    maps_b, units_x = ordered(maps_b, units_x)
    part_x = [exchange_set(which, units_x, choice, dev_count) for which in (0, 1)]
    (part_x, maps_b), got1_a = ordered((part_x, maps_b), got1_a)
    sums_a = partial_sums(maps_a, got1_a)
    sums_a, units_x = ordered(sums_a, units_x)
    got2_a = second_step(sums_a)
    part_x.append(exchange_set(2, units_x, choice, dev_count))
    (part_x, maps_b), got2_a = ordered((part_x, maps_b), got2_a)
    got1_b = first_step(maps_b)
    units_a = columns(maps_a, got1_a, got2_a)
    part_a = [exchange_set(which, units_a, choice, dev_count) for which in (0, 1)]
    part_a, got1_b = ordered(part_a, got1_b)
    sums_b = partial_sums(maps_b, got1_b)
    sums_b, units_a = ordered(sums_b, units_a)
    got2_b = second_step(sums_b)
    part_a.append(exchange_set(2, units_a, choice, dev_count))
    part_a, got2_b = ordered(part_a, got2_b)
    units_b = columns(maps_b, got1_b, got2_b)
    part_b = [exchange_set(which, units_b, choice, dev_count) for which in range(3)]

    coarse_features = merge_features(collect(units_x, part_x), src).T
    coarse_adjacency = merge_tiles(collect(units_a, part_a), src, 0, None)
    coarse_adjacency = merge_tiles(collect(units_b, part_b), src, rows, coarse_adjacency)
    return coarse_adjacency, coarse_features


def solution(mesh):
    in_specs = (
        P("dev", "grp", None),
        P("dev", "grp"),
        P("dev", None),
        P("grp", None),
        P(),
        P(),
        P(),
    )
    out_specs = (P("dev", "grp", None), P("dev", "grp"))
    return jax.shard_map(body, mesh=mesh, in_specs=in_specs, out_specs=out_specs, check_vma=False)
```

```python
import functools
import jax
import jax.numpy as jnp
from jax import lax
from jax.experimental import pallas as pl
from jax.experimental.pallas import tpu as pltpu
from jax.sharding import PartitionSpec as P

TILE = 128
GROUPS = 4
ANY = pl.BlockSpec(memory_space=pl.ANY)
VMEM = pl.BlockSpec(memory_space=pltpu.VMEM)
SMEM = pl.BlockSpec(memory_space=pltpu.SMEM)


def split16(x):
    high = x.astype(jnp.bfloat16)
    low = (x - high.astype(jnp.float32)).astype(jnp.bfloat16)
    return high, low


def sort_blocks(capacity, in_sets, offset_ref, used_ref, slot_ref, where_ref, choice_ref):
    offsets, blocks = used_ref.shape[0], slot_ref.shape[0]
    half = capacity // 2
    for n in range(offsets):
        used_ref[n] = 0
    for p in range(blocks):
        offset = offset_ref[p]
        rank = used_ref[offset]
        slot_ref[p] = offset * capacity + rank
        used_ref[offset] = rank + 1
    for p in range(blocks):
        offset, slot = offset_ref[p], slot_ref[p]
        where_ref[p] = slot
        if in_sets:
            few = jnp.logical_and(used_ref[offset] <= half, offset > 0)
            in_half = capacity * offsets + (offset - 1) * half + slot - offset * capacity
            where_ref[p] = jnp.where(few, in_half, slot)
    for n in range(offsets):
        count = used_ref[n]
        used_ref[n] = jnp.where(count > half, 2, jnp.where(count > 0, 1, 0))
    for n, shifts in enumerate(SETS if in_sets else ()):
        code = jnp.int32(0)
        for i, shift in enumerate(shifts):
            code += used_ref[shift] * 3**i
        choice_ref[n] = code


def head_kernel(step_blocks, chunks, capacity, in_sets, *refs):
    offset_ref, pair_ref, slots_ref, col_ref, x_ref = refs[:5]
    tiles, refs = refs[5 : 5 + 2 * step_blocks], refs[5 + 2 * step_blocks :]
    outs, refs = refs[: 4 * chunks], refs[4 * chunks :]
    used_ref, slot_ref, where_ref, choice_ref, source_ref = refs[:5]
    units, (onehot, held, sem) = refs[5:-3], refs[-3:]
    step, steps = pl.program_id(0), pl.num_programs(0)
    full = (len(units) + 1) // 2

    @pl.when(step == 0)
    def _():
        sort_blocks(capacity, in_sets, offset_ref, used_ref, slot_ref, where_ref, choice_ref)
        group = lax.axis_index("grp")
        keys = []
        for r in range(2):
            owner = jnp.int32(0)
            for h in range(2 * GROUPS):
                owner = jnp.where(pair_ref[h] == 2 * group + r, h // 2, owner)
            keys.append(jnp.bitwise_xor(owner, group) * TILE + slots_ref[r : r + 1, :])
        key = jnp.concatenate(keys + keys, axis=1)
        place = lax.broadcasted_iota(jnp.int32, (GROUPS * TILE, 4 * TILE), 0)
        onehot[...] = (place == key).astype(jnp.float32).astype(jnp.bfloat16)

    here = x_ref.shape[1] // TILE

    @pl.when(step < 2)
    def _():
        lane = lax.broadcasted_iota(jnp.int32, (8, TILE), 1).astype(jnp.float32).astype(jnp.bfloat16)
        place = lax.broadcasted_iota(jnp.int32, (TILE, TILE), 0)
        for j in range(here):
            p = step * here + j
            moves = (place == col_ref[pl.ds(p, 1), :]).astype(jnp.float32).astype(jnp.bfloat16)
            source = lax.dot_general(
                lane, moves, (((1,), (1,)), ((), ())), preferred_element_type=jnp.float32
            )
            source = source[:1].astype(jnp.int32)
            source_ref[pl.ds(p, 1), :] = source
            held[slot_ref[p]] = lanes_of(x_ref[:, j * TILE : (j + 1) * TILE], source)

    @pl.when(step == 2)
    def _():
        write_units(held, units, sem, full, used_ref, lambda copy: copy.start())

    rows = TILE // chunks
    homes = (((1, 0), (0, 0), (1, 1), (0, 1)), ((3, 0), (3, 1), (2, 0), (2, 1)))
    for side in range(2):
        for i in range(0, step_blocks, 2):
            pair = [tile[0] for tile in tiles[side * step_blocks + i : side * step_blocks + i + 2]]
            high, low = split16(jnp.concatenate(pair, axis=1))
            both = jnp.concatenate([high, low], axis=0)
            mapped = jnp.dot(onehot[...], both, preferred_element_type=jnp.float32)
            for m, (array, place) in enumerate(homes[side]):
                for j in range(2):
                    for c in range(chunks):
                        first = m * TILE + c * rows
                        part = mapped[first : first + rows, j * TILE : (j + 1) * TILE]
                        outs[4 * c + array][place, i + j] = part

    @pl.when(step == steps - 1)
    def _():
        write_units(held, units, sem, full, used_ref, lambda copy: copy.wait())


def head(adjacency, features_t, col_slot, row_slot, row_pair, col_offset, chunks, dev_count, capacity, in_sets):
    blocks, own_rows, tile = adjacency.shape
    width = features_t.shape[0]
    side = blocks // 2
    rows = tile // chunks
    step_blocks = 4
    steps = side // step_blocks
    full, size = (dev_count, capacity) if in_sets else (1, capacity * dev_count)
    unit_shapes = [(size, width, tile)] * full + [(size // 2, width, tile)] * (full - 1)

    def at(base, j):
        return pl.BlockSpec((1, own_rows, tile), lambda i: (base + step_blocks * i + j, 0, 0))

    scalars = [(dev_count,), (blocks,), (blocks,), (len(SETS),)]
    outs = pl.pallas_call(
        functools.partial(head_kernel, step_blocks, chunks, capacity, in_sets),
        grid=(steps,),
        out_shape=[jax.ShapeDtypeStruct((2, side, rows, tile), jnp.float32)] * (4 * chunks)
        + [jax.ShapeDtypeStruct(shape, jnp.int32) for shape in scalars]
        + [jax.ShapeDtypeStruct((blocks, tile), jnp.int32)]
        + [jax.ShapeDtypeStruct(shape, jnp.float32) for shape in unit_shapes],
        in_specs=[SMEM, SMEM, VMEM, VMEM]
        + [pl.BlockSpec((width, side * tile), lambda i: (0, jnp.minimum(i, 1)))]
        + [at(0, j) for j in range(step_blocks)]
        + [at(side, j) for j in range(step_blocks)],
        out_specs=[pl.BlockSpec((2, step_blocks, rows, tile), lambda i: (0, i, 0, 0))] * (4 * chunks)
        + [SMEM] * 4
        + [VMEM]
        + [ANY] * len(unit_shapes),
        scratch_shapes=[
            pltpu.VMEM((GROUPS * tile, 4 * tile), jnp.bfloat16),
            pltpu.VMEM((full * size, width, tile), jnp.float32),
            pltpu.SemaphoreType.DMA((len(unit_shapes),)),
        ],
        cost_estimate=pl.CostEstimate(flops=int(2e9), bytes_accessed=16 << 20, transcendentals=0),
        name="head",
    )(col_offset, row_pair, row_slot, col_slot, features_t, *([adjacency] * (2 * step_blocks)))
    maps = [outs[4 * c : 4 * c + 4] for c in range(chunks)]
    return maps, outs[4 * chunks : 4 * chunks + 5], list(outs[4 * chunks + 5 :])


def lanes_of(x, source):
    return jnp.take_along_axis(x, jnp.broadcast_to(source, x.shape), axis=1)


def when_used(n, full, used_ref, copy, act):
    if n == 0:
        act(copy)
    else:
        offset, need = (n, 2) if n < full else (n - full + 1, 1)
        pl.when(used_ref[offset] == need)(lambda: act(copy))


def write_units(held, outs, sem, full, used_ref, act):
    for n, out in enumerate(outs):
        size = out.shape[0]
        at = n * size if n < full else (n - full + 1) * 2 * size
        copy = pltpu.make_async_copy(held.at[pl.ds(at, size)], out, sem.at[n])
        when_used(n, full, used_ref, copy, act)


def columns_kernel(step_blocks, steps, full, used_ref, slot_ref, source_ref, *refs):
    ins, outs, held, sem = refs[:6], refs[6:-2], refs[-2], refs[-1]
    i = pl.program_id(0)
    for side in range(2):
        keep, got1, got2 = ins[3 * side : 3 * side + 3]
        for j in range(step_blocks):
            p = side * steps * step_blocks + i * step_blocks + j
            x = keep[0, j] + got1[0, j] + got2[j]
            held[slot_ref[p]] = lanes_of(x, source_ref[pl.ds(p, 1), :])

    @pl.when(i == steps - 1)
    def _():
        write_units(held, outs, sem, full, used_ref, lambda copy: copy.start())
        write_units(held, outs, sem, full, used_ref, lambda copy: copy.wait())


def unit_outputs(full, size, rows):
    half = full - 1
    shapes = [(size, rows, TILE)] * full + [(size // 2, rows, TILE)] * half
    return dict(
        out_shape=[jax.ShapeDtypeStruct(shape, jnp.float32) for shape in shapes],
        out_specs=[ANY] * (full + half),
        scratch_shapes=[
            pltpu.VMEM((full * size, rows, TILE), jnp.float32),
            pltpu.SemaphoreType.DMA((full + half,)),
        ],
    )


def column_map(keep_x, got1_x, got2_x, keep_y, got1_y, got2_y, source, used, slot, full, size):
    half, rows, tile = got2_x.shape
    step_blocks = 8
    steps = half // step_blocks
    four = pl.BlockSpec((1, step_blocks, rows, tile), lambda i: (0, i, 0, 0))
    three = pl.BlockSpec((step_blocks, rows, tile), lambda i: (i, 0, 0))
    return pl.pallas_call(
        functools.partial(columns_kernel, step_blocks, steps, full),
        grid=(steps,),
        in_specs=[SMEM, SMEM, VMEM] + [four, four, three] * 2,
        cost_estimate=pl.CostEstimate(flops=int(1e9), bytes_accessed=4 << 20, transcendentals=0),
        name="column_map",
        **unit_outputs(full, size, rows),
    )(used, slot, source, keep_x, got1_x, got2_x, keep_y, got1_y, got2_y)


def merge_kernel(full, counts, used_ref, where_ref, pair_ref, *refs):
    pieces, (tiles_out, features_out) = refs[: sum(counts)], refs[sum(counts) : sum(counts) + 2]
    held, sem = refs[sum(counts) + 2 : -1], refs[-1]
    loads = []
    done = 0
    for h, count in zip(held, counts):
        at = 0
        load = []
        for n, piece in enumerate(pieces[done : done + count]):
            size = piece.shape[0]
            load.append(pltpu.make_async_copy(piece, h.at[pl.ds(at, size)], sem.at[done + n]))
            at += size
        loads.append(load)
        done += count
    for load in loads:
        for n, copy in enumerate(load):
            when_used(n, full, used_ref, copy, lambda c: c.start())
    first = 0
    for part, (h, load) in enumerate(zip(held, loads)):
        for n, copy in enumerate(load):
            when_used(n, full, used_ref, copy, lambda c: c.wait())
        for k in range(pair_ref.shape[0] // 2):
            total = h[where_ref[pair_ref[2 * k]]] + h[where_ref[pair_ref[2 * k + 1]]]
            if part == 0:
                features_out[:, k * TILE : (k + 1) * TILE] = total
            else:
                tiles_out[k, first : first + h.shape[1]] = total
        if part > 0:
            first += h.shape[1]


def merge(payloads, used, where, col_pair, full):
    counts = [len(pieces) for pieces in payloads]
    count = col_pair.shape[0] // 2
    width = payloads[0][0].shape[1]
    held = [(sum(p.shape[0] for p in pieces),) + pieces[0].shape[1:] for pieces in payloads]
    return pl.pallas_call(
        functools.partial(merge_kernel, full, counts),
        out_shape=[
            jax.ShapeDtypeStruct((count, TILE, TILE), jnp.float32),
            jax.ShapeDtypeStruct((width, count * TILE), jnp.float32),
        ],
        in_specs=[SMEM, SMEM, SMEM] + [ANY] * sum(counts),
        out_specs=[VMEM, VMEM],
        scratch_shapes=[pltpu.VMEM(shape, jnp.float32) for shape in held]
        + [pltpu.SemaphoreType.DMA((sum(counts),))],
        cost_estimate=pl.CostEstimate(flops=int(1e6), bytes_accessed=5 << 20, transcendentals=0),
        name="merge",
    )(used, where, col_pair, *[piece for pieces in payloads for piece in pieces])


SETS = ((1, 4, 7), (2, 6), (3, 5))


def turn(x, shift, dev_count):
    return lax.ppermute(x, "dev", [(i, (i + shift) % dev_count) for i in range(dev_count)])


def unwritten(shapes):
    return pl.pallas_call(
        lambda *refs: None,
        out_shape=[jax.ShapeDtypeStruct(shape, jnp.float32) for shape in shapes],
        out_specs=[ANY] * len(shapes),
        cost_estimate=pl.CostEstimate(flops=0, bytes_accessed=0, transcendentals=0),
        name="unwritten",
    )()


def exchange_set(which, units, choice, dev_count):
    shifts = SETS[which]
    operands = [units[n] for shift in shifts for n in (shift, dev_count - 1 + shift)]

    def branch(code):
        used = [code // 3**i % 3 for i in range(len(shifts))]
        sent = [(u == 2, u == 1) for u in used]
        sent = [flag for pair in sent for flag in pair]

        def run(*arrays):
            rest = list(unwritten([x.shape for x, flag in zip(arrays, sent) if not flag]))
            got = []
            for n, (array, flag) in enumerate(zip(arrays, sent)):
                got.append(turn(array, shifts[n // 2], dev_count) if flag else rest.pop(0))
            return got

        return run

    return lax.switch(choice[which], [branch(c) for c in range(3 ** len(shifts))], *operands)


def exchange_all(blocks, capacity, dev_count):
    me = lax.axis_index("dev")
    ids = jnp.arange(dev_count * capacity, dtype=jnp.int32)
    away, place = ids // capacity, ids % capacity
    send = jnp.take(blocks, (away - me) % dev_count * capacity + place, axis=0)
    got = lax.all_to_all(send, "dev", split_axis=0, concat_axis=0, tiled=True)
    return jnp.take(got, (me - away) % dev_count * capacity + place, axis=0)


def ordered(first, then):
    first, then = lax.optimization_barrier((first, then))
    return first, then


def body(adjacency, features, col_slot, row_slot, row_pair, col_pair, col_offset):
    dev_count = lax.axis_size("dev")
    blocks = adjacency.shape[0]
    capacity = 2 * blocks // dev_count
    in_sets = dev_count == 8
    full, size = (dev_count, capacity) if in_sets else (1, capacity * dev_count)

    (maps_a, maps_b), (used, slot, where, choice, source), units_x = head(
        adjacency, features.T, col_slot, row_slot, row_pair, col_offset, 2, dev_count, capacity, in_sets
    )

    x_side = [(g, g ^ 1) for g in range(GROUPS)]
    y_side = [(g, g ^ 2) for g in range(GROUPS)]

    def first_step(maps):
        return lax.ppermute(maps[0], "grp", x_side), lax.ppermute(maps[2], "grp", y_side)

    def partial_sums(maps, got):
        return maps[1][1] + got[0][1], maps[3][1] + got[1][1]

    def second_step(sums):
        return lax.ppermute(sums[0], "grp", y_side), lax.ppermute(sums[1], "grp", x_side)

    def columns(maps, got1, got2):
        return column_map(
            maps[1], got1[0], got2[0], maps[3], got1[1], got2[1], source, used, slot, full, size
        )

    got1_a = first_step(maps_a)
    if not in_sets:
        payloads = [[exchange_all(units_x[0], capacity, dev_count)]]
        for maps, got1 in ((maps_a, got1_a), (maps_b, first_step(maps_b))):
            units = columns(maps, got1, second_step(partial_sums(maps, got1)))
            payloads.append([exchange_all(units[0], capacity, dev_count)])
        coarse_adjacency, coarse_features = merge(payloads, used, where, col_pair, full)
        return coarse_adjacency, coarse_features.T

    def collect(units, parts):
        pieces = list(units)
        for shifts, part in zip(SETS, parts):
            for i, shift in enumerate(shifts):
                pieces[shift], pieces[dev_count - 1 + shift] = part[2 * i], part[2 * i + 1]
        return pieces

    part_x = [exchange_set(which, units_x, choice, dev_count) for which in (0, 1)]
    (part_x, maps_b), got1_a = ordered((part_x, maps_b), got1_a)
    sums_a = partial_sums(maps_a, got1_a)
    sums_a, units_x = ordered(sums_a, units_x)
    got2_a = second_step(sums_a)
    part_x.append(exchange_set(2, units_x, choice, dev_count))
    (part_x, maps_b), got2_a = ordered((part_x, maps_b), got2_a)
    got1_b = first_step(maps_b)
    units_a = columns(maps_a, got1_a, got2_a)
    part_a = [exchange_set(which, units_a, choice, dev_count) for which in (0, 1)]
    part_a, got1_b = ordered(part_a, got1_b)
    sums_b = partial_sums(maps_b, got1_b)
    sums_b, units_a = ordered(sums_b, units_a)
    got2_b = second_step(sums_b)
    part_a.append(exchange_set(2, units_a, choice, dev_count))
    part_a, got2_b = ordered(part_a, got2_b)
    units_b = columns(maps_b, got1_b, got2_b)
    part_b = [exchange_set(which, units_b, choice, dev_count) for which in range(3)]

    payloads = [collect(*each) for each in ((units_x, part_x), (units_a, part_a), (units_b, part_b))]
    coarse_adjacency, coarse_features = merge(payloads, used, where, col_pair, full)
    return coarse_adjacency, coarse_features.T


def solution(mesh):
    in_specs = (
        P("dev", "grp", None),
        P("dev", "grp"),
        P("dev", None),
        P("grp", None),
        P(),
        P(),
        P(),
    )
    out_specs = (P("dev", "grp", None), P("dev", "grp"))
    return jax.shard_map(body, mesh=mesh, in_specs=in_specs, out_specs=out_specs, check_vma=False)
```

```python
import functools
import itertools
import jax
import jax.numpy as jnp
from jax import lax
from jax.experimental import pallas as pl
from jax.experimental.pallas import tpu as pltpu
from jax.sharding import PartitionSpec as P

TILE = 128
GROUPS = 4
ANY = pl.BlockSpec(memory_space=pl.ANY)
VMEM = pl.BlockSpec(memory_space=pltpu.VMEM)
SMEM = pl.BlockSpec(memory_space=pltpu.SMEM)


def split16(x):
    high = x.astype(jnp.bfloat16)
    low = (x - high.astype(jnp.float32)).astype(jnp.bfloat16)
    return high, low


def sort_blocks(capacity, in_sets, offset_ref, used_refs, slot_ref, where_refs, choices):
    offsets, blocks = used_refs[0].shape[0], slot_ref.shape[0]
    half = capacity // 2
    counts = used_refs[0]
    for n in range(offsets):
        counts[n] = 0
    for p in range(blocks):
        offset = offset_ref[p]
        rank = counts[offset]
        slot_ref[p] = offset * capacity + rank
        counts[offset] = rank + 1
    for p in range(blocks):
        offset, slot = offset_ref[p], slot_ref[p]
        few = jnp.logical_and(counts[offset] <= half, offset > 0)
        in_half = capacity * offsets + (offset - 1) * half + slot - offset * capacity
        for where_ref, (_, whole) in zip(where_refs, PLANS):
            where_ref[p] = slot
            if in_sets:
                halved = few
                for n in whole:
                    halved = jnp.logical_and(halved, offset != n)
                where_ref[p] = jnp.where(halved, in_half, slot)
    for n in range(offsets):
        count = counts[n]
        for used_ref, (_, whole) in zip(used_refs[::-1], PLANS[::-1]):
            some = 2 if in_sets and n in whole else 1
            used_ref[n] = jnp.where(count > half, 2, jnp.where(count > 0, some, 0))
    done = 0
    for used_ref, (sets, whole) in zip(used_refs, PLANS):
        for shifts in sets if in_sets else ():
            code, weight = jnp.int32(0), 1
            for shift in shifts:
                code += (used_ref[shift] // 2 if shift in whole else used_ref[shift]) * weight
                weight *= 2 if shift in whole else 3
            choices[done][0] = code
            done += 1


def head_kernel(chunks, capacity, in_sets, *refs):
    offset_ref, pair_ref, slots_ref, col_ref, x_ref, tiles = refs[:6]
    outs, refs = refs[6 : 6 + 3 * chunks], refs[6 + 3 * chunks :]
    used_refs, where_refs, slot_ref, refs = refs[:2], refs[2:4], refs[4], refs[5:]
    choices, refs = refs[:SET_COUNT], refs[SET_COUNT:]
    source_ref, units, (onehot, held, sem) = refs[0], refs[1:-3], refs[-3:]
    step, steps = pl.program_id(0), pl.num_programs(0)
    full, used_ref = (len(units) + 1) // 2, used_refs[0]

    @pl.when(step == 0)
    def _():
        sort_blocks(capacity, in_sets, offset_ref, used_refs, slot_ref, where_refs, choices)
        group = lax.axis_index("grp")
        odd = lax.rem(lax.axis_index("dev"), 2) == 1
        keys = []
        for r in range(2):
            owner = jnp.int32(0)
            for h in range(2 * GROUPS):
                owner = jnp.where(pair_ref[h] == 2 * group + r, h // 2, owner)
            away = jnp.bitwise_xor(owner, group)
            away = jnp.where(odd, away // 2 + 2 * lax.rem(away, 2), away)
            keys.append(away * TILE + slots_ref[r : r + 1, :])
        key = jnp.concatenate(keys + keys, axis=1)
        place = lax.broadcasted_iota(jnp.int32, (GROUPS * TILE, 4 * TILE), 0)
        onehot[...] = (place == key).astype(jnp.float32).astype(jnp.bfloat16)

    here = x_ref.shape[1] // TILE

    @pl.when(step < 2)
    def _():
        lane = lax.broadcasted_iota(jnp.int32, (8, TILE), 1).astype(jnp.float32).astype(jnp.bfloat16)
        place = lax.broadcasted_iota(jnp.int32, (TILE, TILE), 0)
        for j in range(here):
            p = step * here + j
            moves = (place == col_ref[pl.ds(p, 1), :]).astype(jnp.float32).astype(jnp.bfloat16)
            source = lax.dot_general(
                lane, moves, (((1,), (1,)), ((), ())), preferred_element_type=jnp.float32
            )
            source = source[:1].astype(jnp.int32)
            source_ref[pl.ds(p, 1), :] = source
            held[slot_ref[p]] = lanes_of(x_ref[:, j * TILE : (j + 1) * TILE], source)

    @pl.when(step == 2)
    def _():
        write_units(held, units, sem, full, used_ref, lambda copy: copy.start())

    rows = TILE // chunks
    for i in range(0, tiles.shape[0], 2):
        high, low = split16(jnp.concatenate([tiles[i], tiles[i + 1]], axis=1))
        both = jnp.concatenate([high, low], axis=0)
        mapped = jnp.dot(onehot[...], both, preferred_element_type=jnp.float32)
        for j in range(2):
            for c in range(chunks):
                send, keep, add = outs[3 * c : 3 * c + 3]
                part = [
                    mapped[m * TILE + c * rows : m * TILE + (c + 1) * rows, j * TILE : (j + 1) * TILE]
                    for m in range(GROUPS)
                ]
                keep[i + j], send[0, i + j], add[i + j], send[1, i + j] = part

    @pl.when(step == steps - 1)
    def _():
        write_units(held, units, sem, full, used_ref, lambda copy: copy.wait())


def head(adjacency, features_t, col_slot, row_slot, row_pair, col_offset, chunks, dev_count, capacity, in_sets):
    blocks, own_rows, tile = adjacency.shape
    width = features_t.shape[0]
    rows = tile // chunks
    step_blocks = blocks // 4
    full, size = (dev_count, capacity) if in_sets else (1, capacity * dev_count)
    unit_shapes = [(size, width, tile)] * full + [(size // 2, width, tile)] * (full - 1)

    two = jax.ShapeDtypeStruct((2, blocks, rows, tile), jnp.float32)
    one = jax.ShapeDtypeStruct((blocks, rows, tile), jnp.float32)
    two_spec = pl.BlockSpec((2, step_blocks, rows, tile), lambda i: (0, i, 0, 0))
    one_spec = pl.BlockSpec((step_blocks, rows, tile), lambda i: (i, 0, 0))
    scalars = [(dev_count,)] * 2 + [(blocks,)] * 3 + [(1,)] * SET_COUNT
    outs = pl.pallas_call(
        functools.partial(head_kernel, chunks, capacity, in_sets),
        grid=(blocks // step_blocks,),
        out_shape=[two, one, one] * chunks
        + [jax.ShapeDtypeStruct(shape, jnp.int32) for shape in scalars]
        + [jax.ShapeDtypeStruct((blocks, tile), jnp.int32)]
        + [jax.ShapeDtypeStruct(shape, jnp.float32) for shape in unit_shapes],
        in_specs=[SMEM, SMEM, VMEM, VMEM]
        + [pl.BlockSpec((width, blocks // 2 * tile), lambda i: (0, jnp.minimum(i, 1)))]
        + [pl.BlockSpec((step_blocks, own_rows, tile), lambda i: (i, 0, 0))],
        out_specs=[two_spec, one_spec, one_spec] * chunks
        + [SMEM] * len(scalars)
        + [VMEM]
        + [ANY] * len(unit_shapes),
        scratch_shapes=[
            pltpu.VMEM((GROUPS * tile, 4 * tile), jnp.bfloat16),
            pltpu.VMEM((full * size, width, tile), jnp.float32),
            pltpu.SemaphoreType.DMA((len(unit_shapes),)),
        ],
        cost_estimate=pl.CostEstimate(flops=int(2e9), bytes_accessed=16 << 20, transcendentals=0),
        name="head",
    )(col_offset, row_pair, row_slot, col_slot, features_t, adjacency)
    maps, outs = [outs[3 * c : 3 * c + 3] for c in range(chunks)], outs[3 * chunks :]
    used, where, slot = outs[:2], outs[2:4], outs[4]
    choice = [each[0] for each in outs[5 : 5 + SET_COUNT]]
    return maps, used, slot, where, choice, outs[5 + SET_COUNT], list(outs[6 + SET_COUNT :])


def lanes_of(x, source):
    return jnp.take_along_axis(x, jnp.broadcast_to(source, x.shape), axis=1)


def when_used(n, full, used_ref, copy, act):
    if n == 0:
        act(copy)
    else:
        offset, need = (n, 2) if n < full else (n - full + 1, 1)
        pl.when(used_ref[offset] == need)(lambda: act(copy))


def write_units(held, outs, sem, full, used_ref, act):
    for n, out in enumerate(outs):
        size = out.shape[0]
        at = n * size if n < full else (n - full + 1) * 2 * size
        copy = pltpu.make_async_copy(held.at[pl.ds(at, size)], out, sem.at[n])
        when_used(n, full, used_ref, copy, act)


def columns_kernel(step_blocks, steps, full, used_ref, slot_ref, source_ref, keep, got1, got2, *refs):
    outs, held, sem = refs[:-2], refs[-2], refs[-1]
    i = pl.program_id(0)
    for j in range(step_blocks):
        p = i * step_blocks + j
        x = keep[j] + got1[0, j] + got2[j]
        held[slot_ref[p]] = lanes_of(x, source_ref[pl.ds(p, 1), :])

    @pl.when(i == steps - 1)
    def _():
        write_units(held, outs, sem, full, used_ref, lambda copy: copy.start())
        write_units(held, outs, sem, full, used_ref, lambda copy: copy.wait())


def unit_outputs(full, size, rows):
    half = full - 1
    shapes = [(size, rows, TILE)] * full + [(size // 2, rows, TILE)] * half
    return dict(
        out_shape=[jax.ShapeDtypeStruct(shape, jnp.float32) for shape in shapes],
        out_specs=[ANY] * (full + half),
        scratch_shapes=[
            pltpu.VMEM((full * size, rows, TILE), jnp.float32),
            pltpu.SemaphoreType.DMA((full + half,)),
        ],
    )


def column_map(keep, got1, got2, source, used, slot, full, size):
    blocks, rows, tile = keep.shape
    step_blocks = blocks // 2
    steps = blocks // step_blocks
    one = pl.BlockSpec((step_blocks, rows, tile), lambda i: (i, 0, 0))
    two = pl.BlockSpec((1, step_blocks, rows, tile), lambda i: (0, i, 0, 0))
    return pl.pallas_call(
        functools.partial(columns_kernel, step_blocks, steps, full),
        grid=(steps,),
        in_specs=[SMEM, SMEM, VMEM, one, two, one],
        cost_estimate=pl.CostEstimate(flops=int(1e9), bytes_accessed=4 << 20, transcendentals=0),
        name="column_map",
        **unit_outputs(full, size, rows),
    )(used, slot, source, keep, got1, got2)


def merge_kernel(full, counts, plans, pair_ref, *refs):
    plan_refs, refs = refs[:4], refs[4:]
    pieces, (tiles_out, features_out) = refs[: sum(counts)], refs[sum(counts) : sum(counts) + 2]
    held, sem = refs[sum(counts) + 2 : -1], refs[-1]
    loads = []
    done = 0
    for h, count in zip(held, counts):
        at = 0
        load = []
        for n, piece in enumerate(pieces[done : done + count]):
            size = piece.shape[0]
            load.append(pltpu.make_async_copy(piece, h.at[pl.ds(at, size)], sem.at[done + n]))
            at += size
        loads.append(load)
        done += count
    for plan, load in zip(plans, loads):
        for n, copy in enumerate(load):
            when_used(n, full, plan_refs[plan], copy, lambda c: c.start())
    first = 0
    for part, (plan, h, load) in enumerate(zip(plans, held, loads)):
        used_ref, where_ref = plan_refs[plan], plan_refs[2 + plan]
        for n, copy in enumerate(load):
            when_used(n, full, used_ref, copy, lambda c: c.wait())
        for k in range(pair_ref.shape[0] // 2):
            total = h[where_ref[pair_ref[2 * k]]] + h[where_ref[pair_ref[2 * k + 1]]]
            if part == 0:
                features_out[:, k * TILE : (k + 1) * TILE] = total
            else:
                tiles_out[k, first : first + h.shape[1]] = total
        if part > 0:
            first += h.shape[1]


def merge(payloads, plans, used, where, col_pair, full):
    counts = [len(pieces) for pieces in payloads]
    count = col_pair.shape[0] // 2
    width = payloads[0][0].shape[1]
    held = [(sum(p.shape[0] for p in pieces),) + pieces[0].shape[1:] for pieces in payloads]
    return pl.pallas_call(
        functools.partial(merge_kernel, full, counts, plans),
        out_shape=[
            jax.ShapeDtypeStruct((count, TILE, TILE), jnp.float32),
            jax.ShapeDtypeStruct((width, count * TILE), jnp.float32),
        ],
        in_specs=[SMEM] * 5 + [ANY] * sum(counts),
        out_specs=[VMEM, VMEM],
        scratch_shapes=[pltpu.VMEM(shape, jnp.float32) for shape in held]
        + [pltpu.SemaphoreType.DMA((sum(counts),))],
        cost_estimate=pl.CostEstimate(flops=int(1e6), bytes_accessed=5 << 20, transcendentals=0),
        name="merge",
    )(col_pair, *used, *where, *[piece for pieces in payloads for piece in pieces])


BESIDE = ((2, 6), (1, 4, 7), (3, 5))
LAST = ((3, 4, 5), (1, 7, 2, 6))
PLANS = ((BESIDE, ()), (LAST, (1, 7)))
SET_COUNT = len(BESIDE) + len(LAST)


def turn(x, shift, dev_count):
    return lax.ppermute(x, "dev", [(i, (i + shift) % dev_count) for i in range(dev_count)])


def unwritten(shapes):
    return pl.pallas_call(
        lambda *refs: None,
        out_shape=[jax.ShapeDtypeStruct(shape, jnp.float32) for shape in shapes],
        out_specs=[ANY] * len(shapes),
        cost_estimate=pl.CostEstimate(flops=0, bytes_accessed=0, transcendentals=0),
        name="unwritten",
    )()


def exchange_set(shifts, whole, units, choice, dev_count):
    operands = [units[n] for shift in shifts for n in (shift, dev_count - 1 + shift)]

    levels = [(0, 2) if shift in whole else (0, 1, 2) for shift in shifts]
    codes = [code[::-1] for code in itertools.product(*levels[::-1])]

    def branch(used):
        sent = [(u == 2, u == 1) for u in used]
        sent = [flag for pair in sent for flag in pair]

        def run(*arrays):
            rest = list(unwritten([x.shape for x, flag in zip(arrays, sent) if not flag]))
            got = []
            for n, (array, flag) in enumerate(zip(arrays, sent)):
                got.append(turn(array, shifts[n // 2], dev_count) if flag else rest.pop(0))
            return got

        return run

    return lax.switch(choice, [branch(code) for code in codes], *operands)


def exchange_all(blocks, capacity, dev_count):
    me = lax.axis_index("dev")
    ids = jnp.arange(dev_count * capacity, dtype=jnp.int32)
    away, place = ids // capacity, ids % capacity
    send = jnp.take(blocks, (away - me) % dev_count * capacity + place, axis=0)
    got = lax.all_to_all(send, "dev", split_axis=0, concat_axis=0, tiled=True)
    return jnp.take(got, (me - away) % dev_count * capacity + place, axis=0)


def ordered(first, then):
    first, then = lax.optimization_barrier((first, then))
    return first, then


def body(adjacency, features, col_slot, row_slot, row_pair, col_pair, col_offset):
    dev_count = lax.axis_size("dev")
    blocks = adjacency.shape[0]
    capacity = 2 * blocks // dev_count
    in_sets = dev_count == 8
    full, size = (dev_count, capacity) if in_sets else (1, capacity * dev_count)

    (maps_a, maps_b), used, slot, where, choice, source, units_x = head(
        adjacency, features.T, col_slot, row_slot, row_pair, col_offset, 2, dev_count, capacity, in_sets
    )

    def over_grp(x, distance):
        pairs = []
        for g in range(GROUPS):
            for d in range(dev_count):
                to = g ^ (distance if d % 2 == 0 else 3 - distance)
                pairs.append((g * dev_count + d, to * dev_count + d))
        return lax.ppermute(x, ("grp", "dev"), pairs)

    def columns(maps, got1, got2, plan):
        return column_map(maps[1], got1, got2, source, used[plan], slot, full, size)

    got1_a = over_grp(maps_a[0], 1)
    if not in_sets:
        payloads = [[exchange_all(units_x[0], capacity, dev_count)]]
        for maps, got1 in ((maps_a, got1_a), (maps_b, over_grp(maps_b[0], 1))):
            units = columns(maps, got1, over_grp(maps[2] + got1[1], 2), 0)
            payloads.append([exchange_all(units[0], capacity, dev_count)])
        coarse_adjacency, coarse_features = merge(payloads, (0, 0, 0), used, where, col_pair, full)
        return coarse_adjacency, coarse_features.T

    def collect(units, sets, parts):
        pieces = list(units)
        for shifts, part in zip(sets, parts):
            for i, shift in enumerate(shifts):
                pieces[shift], pieces[dev_count - 1 + shift] = part[2 * i], part[2 * i + 1]
        return pieces

    def exchange(units, plan, which):
        sets, whole = PLANS[plan]
        return [
            exchange_set(sets[n], whole, units, choice[plan * len(BESIDE) + n], dev_count) for n in which
        ]

    part_x = exchange(units_x, 0, (0, 1))
    (part_x, maps_b), got1_a = ordered((part_x, maps_b), got1_a)
    sum_a = maps_a[2] + got1_a[1]
    sum_a, units_x = ordered(sum_a, units_x)
    got2_a = over_grp(sum_a, 2)
    part_x += exchange(units_x, 0, (2,))
    (part_x, maps_b), got2_a = ordered((part_x, maps_b), got2_a)
    got1_b = over_grp(maps_b[0], 1)
    units_a = columns(maps_a, got1_a, got2_a, 0)
    part_a = exchange(units_a, 0, (0, 1))
    part_a, got1_b = ordered(part_a, got1_b)
    sum_b = maps_b[2] + got1_b[1]
    sum_b, units_a = ordered(sum_b, units_a)
    got2_b = over_grp(sum_b, 2)
    part_a += exchange(units_a, 0, (2,))
    part_a, got2_b = ordered(part_a, got2_b)
    units_b = columns(maps_b, got1_b, got2_b, 1)
    part_b = exchange(units_b, 1, (0, 1))

    payloads = [
        collect(units_x, BESIDE, part_x),
        collect(units_a, BESIDE, part_a),
        collect(units_b, LAST, part_b),
    ]
    coarse_adjacency, coarse_features = merge(payloads, (0, 0, 1), used, where, col_pair, full)
    return coarse_adjacency, coarse_features.T


def solution(mesh):
    in_specs = (
        P("dev", "grp", None),
        P("dev", "grp"),
        P("dev", None),
        P("grp", None),
        P(),
        P(),
        P(),
    )
    out_specs = (P("dev", "grp", None), P("dev", "grp"))
    return jax.shard_map(body, mesh=mesh, in_specs=in_specs, out_specs=out_specs, check_vma=False)
```

```python
import functools
import itertools
import jax
import jax.numpy as jnp
from jax import lax
from jax.experimental import pallas as pl
from jax.experimental.pallas import tpu as pltpu
from jax.sharding import PartitionSpec as P

TILE = 128
GROUPS = 4
ANY = pl.BlockSpec(memory_space=pl.ANY)
VMEM = pl.BlockSpec(memory_space=pltpu.VMEM)
SMEM = pl.BlockSpec(memory_space=pltpu.SMEM)


def split16(x):
    high = x.astype(jnp.bfloat16)
    low = (x - high.astype(jnp.float32)).astype(jnp.bfloat16)
    return high, low


def sort_blocks(capacity, in_sets, offset_ref, used_refs, slot_ref, where_refs, choice_ref):
    offsets, blocks = used_refs[0].shape[0], slot_ref.shape[0]
    half = capacity // 2
    counts = used_refs[0]
    for n in range(offsets):
        counts[n] = 0
    for p in range(blocks):
        offset = offset_ref[p]
        rank = counts[offset]
        slot_ref[p] = offset * capacity + rank
        counts[offset] = rank + 1
    for p in range(blocks):
        offset, slot = offset_ref[p], slot_ref[p]
        few = jnp.logical_and(counts[offset] <= half, offset > 0)
        in_half = capacity * offsets + (offset - 1) * half + slot - offset * capacity
        for where_ref, (_, whole) in zip(where_refs, PLANS):
            where_ref[p] = slot
            if in_sets:
                halved = few
                for n in whole:
                    halved = jnp.logical_and(halved, offset != n)
                where_ref[p] = jnp.where(halved, in_half, slot)
    for n in range(offsets):
        count = counts[n]
        for used_ref, (_, whole) in zip(used_refs[::-1], PLANS[::-1]):
            some = 2 if in_sets and n in whole else 1
            used_ref[n] = jnp.where(count > half, 2, jnp.where(count > 0, some, 0))
    packed, at = jnp.int32(0), 0
    for used_ref, (sets, whole) in zip(used_refs, PLANS):
        for shifts in sets if in_sets else ():
            code, weight = jnp.int32(0), 1
            for shift in shifts:
                code += (used_ref[shift] // 2 if shift in whole else used_ref[shift]) * weight
                weight *= 2 if shift in whole else 3
            packed += code * 2**at
            at += CODE_BITS
    choice_ref[0] = packed


def head_kernel(chunks, capacity, in_sets, *refs):
    offset_ref, pair_ref, slots_ref, col_ref, x_ref, tiles = refs[:6]
    outs, refs = refs[6 : 6 + 3 * chunks], refs[6 + 3 * chunks :]
    used_refs, where_refs, slot_ref, choice_ref, refs = refs[:2], refs[2:4], refs[4], refs[5], refs[6:]
    source_ref, units, (onehot, held, sem) = refs[0], refs[1:-3], refs[-3:]
    step, steps = pl.program_id(0), pl.num_programs(0)
    full, used_ref = (len(units) + 1) // 2, used_refs[0]

    @pl.when(step == 0)
    def _():
        sort_blocks(capacity, in_sets, offset_ref, used_refs, slot_ref, where_refs, choice_ref)
        group = lax.axis_index("grp")
        odd = lax.rem(lax.axis_index("dev"), 2) == 1
        keys = []
        for r in range(2):
            owner = jnp.int32(0)
            for h in range(2 * GROUPS):
                owner = jnp.where(pair_ref[h] == 2 * group + r, h // 2, owner)
            away = jnp.bitwise_xor(owner, group)
            away = jnp.where(odd, away // 2 + 2 * lax.rem(away, 2), away)
            keys.append(away * TILE + slots_ref[r : r + 1, :])
        key = jnp.concatenate(keys, axis=1)
        place = lax.broadcasted_iota(jnp.int32, (GROUPS * TILE, 2 * TILE), 0)
        moves = (place == key).astype(jnp.float32).astype(jnp.bfloat16)
        onehot[:, : 2 * TILE] = moves
        onehot[:, 2 * TILE :] = moves

    here = x_ref.shape[1] // TILE

    @pl.when(step == 0)
    def _():
        lane = lax.broadcasted_iota(jnp.int32, (8, TILE), 1).astype(jnp.float32).astype(jnp.bfloat16)
        place = lax.broadcasted_iota(jnp.int32, (TILE, TILE), 0)
        for j in range(here):
            p = j
            moves = (place == col_ref[pl.ds(p, 1), :]).astype(jnp.float32).astype(jnp.bfloat16)
            source = lax.dot_general(
                lane, moves, (((1,), (1,)), ((), ())), preferred_element_type=jnp.float32
            )
            source = source[:1].astype(jnp.int32)
            source_ref[pl.ds(p, 1), :] = source
            held[slot_ref[p]] = lanes_of(x_ref[:, j * TILE : (j + 1) * TILE], source)

    @pl.when(step == 0)
    def _():
        write_units(held, units, sem, full, used_ref, lambda copy: copy.start())

    rows = TILE // chunks
    for i in range(0, tiles.shape[0], 2):
        high, low = split16(jnp.concatenate([tiles[i], tiles[i + 1]], axis=1))
        both = jnp.concatenate([high, low], axis=0)
        mapped = jnp.dot(onehot[...], both, preferred_element_type=jnp.float32)
        for j in range(2):
            for c in range(chunks):
                send, keep, add = outs[3 * c : 3 * c + 3]
                part = [
                    mapped[m * TILE + c * rows : m * TILE + (c + 1) * rows, j * TILE : (j + 1) * TILE]
                    for m in range(GROUPS)
                ]
                keep[i + j], send[0, i + j], add[i + j], send[1, i + j] = part

    @pl.when(step == steps - 1)
    def _():
        write_units(held, units, sem, full, used_ref, lambda copy: copy.wait())


def head(adjacency, features_t, col_slot, row_slot, row_pair, col_offset, chunks, dev_count, capacity, in_sets):
    blocks, own_rows, tile = adjacency.shape
    width = features_t.shape[0]
    rows = tile // chunks
    step_blocks = blocks // 2
    full, size = (dev_count, capacity) if in_sets else (1, capacity * dev_count)
    unit_shapes = [(size, width, tile)] * full + [(size // 2, width, tile)] * (full - 1)

    two = jax.ShapeDtypeStruct((2, blocks, rows, tile), jnp.float32)
    one = jax.ShapeDtypeStruct((blocks, rows, tile), jnp.float32)
    two_spec = pl.BlockSpec((2, step_blocks, rows, tile), lambda i: (0, i, 0, 0))
    one_spec = pl.BlockSpec((step_blocks, rows, tile), lambda i: (i, 0, 0))
    scalars = [(dev_count,)] * 2 + [(blocks,)] * 3 + [(1,)]
    outs = pl.pallas_call(
        functools.partial(head_kernel, chunks, capacity, in_sets),
        grid=(blocks // step_blocks,),
        out_shape=[two, one, one] * chunks
        + [jax.ShapeDtypeStruct(shape, jnp.int32) for shape in scalars]
        + [jax.ShapeDtypeStruct((blocks, tile), jnp.int32)]
        + [jax.ShapeDtypeStruct(shape, jnp.float32) for shape in unit_shapes],
        in_specs=[SMEM, SMEM, VMEM, VMEM]
        + [pl.BlockSpec((width, blocks * tile), lambda i: (0, 0))]
        + [pl.BlockSpec((step_blocks, own_rows, tile), lambda i: (i, 0, 0))],
        out_specs=[two_spec, one_spec, one_spec] * chunks
        + [SMEM] * len(scalars)
        + [VMEM]
        + [ANY] * len(unit_shapes),
        scratch_shapes=[
            pltpu.VMEM((GROUPS * tile, 4 * tile), jnp.bfloat16),
            pltpu.VMEM((full * size, width, tile), jnp.float32),
            pltpu.SemaphoreType.DMA((len(unit_shapes),)),
        ],
        compiler_params=pltpu.CompilerParams(vmem_limit_bytes=60 << 20),
        cost_estimate=pl.CostEstimate(flops=int(2e9), bytes_accessed=16 << 20, transcendentals=0),
        name="head",
    )(col_offset, row_pair, row_slot, col_slot, features_t, adjacency)
    maps, outs = [outs[3 * c : 3 * c + 3] for c in range(chunks)], outs[3 * chunks :]
    used, where, slot = outs[:2], outs[2:4], outs[4]
    return maps, used, slot, where, outs[5][0], outs[6], list(outs[7:])


def lanes_of(x, source):
    return jnp.take_along_axis(x, jnp.broadcast_to(source, x.shape), axis=1)


def when_used(n, full, used_ref, copy, act):
    if n == 0:
        act(copy)
    else:
        offset, need = (n, 2) if n < full else (n - full + 1, 1)
        pl.when(used_ref[offset] == need)(lambda: act(copy))


def write_units(held, outs, sem, full, used_ref, act):
    for n, out in enumerate(outs):
        size = out.shape[0]
        at = n * size if n < full else (n - full + 1) * 2 * size
        copy = pltpu.make_async_copy(held.at[pl.ds(at, size)], out, sem.at[n])
        when_used(n, full, used_ref, copy, act)


def columns_kernel(step_blocks, steps, full, used_ref, slot_ref, source_ref, keep, got1, got2, *refs):
    outs, held, sem = refs[:-2], refs[-2], refs[-1]
    i = pl.program_id(0)
    for j in range(step_blocks):
        p = i * step_blocks + j
        x = keep[j] + got1[0, j] + got2[j]
        held[slot_ref[p]] = lanes_of(x, source_ref[pl.ds(p, 1), :])

    @pl.when(i == steps - 1)
    def _():
        write_units(held, outs, sem, full, used_ref, lambda copy: copy.start())
        write_units(held, outs, sem, full, used_ref, lambda copy: copy.wait())


def unit_outputs(full, size, rows):
    half = full - 1
    shapes = [(size, rows, TILE)] * full + [(size // 2, rows, TILE)] * half
    return dict(
        out_shape=[jax.ShapeDtypeStruct(shape, jnp.float32) for shape in shapes],
        out_specs=[ANY] * (full + half),
        scratch_shapes=[
            pltpu.VMEM((full * size, rows, TILE), jnp.float32),
            pltpu.SemaphoreType.DMA((full + half,)),
        ],
    )


def column_map(keep, got1, got2, source, used, slot, full, size):
    blocks, rows, tile = keep.shape
    step_blocks = blocks // 2
    steps = blocks // step_blocks
    one = pl.BlockSpec((step_blocks, rows, tile), lambda i: (i, 0, 0))
    two = pl.BlockSpec((1, step_blocks, rows, tile), lambda i: (0, i, 0, 0))
    return pl.pallas_call(
        functools.partial(columns_kernel, step_blocks, steps, full),
        grid=(steps,),
        in_specs=[SMEM, SMEM, VMEM, one, two, one],
        cost_estimate=pl.CostEstimate(flops=int(1e9), bytes_accessed=4 << 20, transcendentals=0),
        name="column_map",
        **unit_outputs(full, size, rows),
    )(used, slot, source, keep, got1, got2)


def merge_kernel(full, counts, plans, pair_ref, *refs):
    plan_refs, refs = refs[:4], refs[4:]
    pieces, (tiles_out, features_out) = refs[: sum(counts)], refs[sum(counts) : sum(counts) + 2]
    held, sem = refs[sum(counts) + 2 : -1], refs[-1]
    loads = []
    done = 0
    for h, count in zip(held, counts):
        at = 0
        load = []
        for n, piece in enumerate(pieces[done : done + count]):
            size = piece.shape[0]
            load.append(pltpu.make_async_copy(piece, h.at[pl.ds(at, size)], sem.at[done + n]))
            at += size
        loads.append(load)
        done += count
    for plan, load in zip(plans, loads):
        for n, copy in enumerate(load):
            when_used(n, full, plan_refs[plan], copy, lambda c: c.start())
    first = 0
    for part, (plan, h, load) in enumerate(zip(plans, held, loads)):
        used_ref, where_ref = plan_refs[plan], plan_refs[2 + plan]
        for n, copy in enumerate(load):
            when_used(n, full, used_ref, copy, lambda c: c.wait())
        for k in range(pair_ref.shape[0] // 2):
            total = h[where_ref[pair_ref[2 * k]]] + h[where_ref[pair_ref[2 * k + 1]]]
            if part == 0:
                features_out[:, k * TILE : (k + 1) * TILE] = total
            else:
                tiles_out[k, first : first + h.shape[1]] = total
        if part > 0:
            first += h.shape[1]


def merge(payloads, plans, used, where, col_pair, full):
    counts = [len(pieces) for pieces in payloads]
    count = col_pair.shape[0] // 2
    width = payloads[0][0].shape[1]
    held = [(sum(p.shape[0] for p in pieces),) + pieces[0].shape[1:] for pieces in payloads]
    return pl.pallas_call(
        functools.partial(merge_kernel, full, counts, plans),
        out_shape=[
            jax.ShapeDtypeStruct((count, TILE, TILE), jnp.float32),
            jax.ShapeDtypeStruct((width, count * TILE), jnp.float32),
        ],
        in_specs=[SMEM] * 5 + [ANY] * sum(counts),
        out_specs=[VMEM, VMEM],
        scratch_shapes=[pltpu.VMEM(shape, jnp.float32) for shape in held]
        + [pltpu.SemaphoreType.DMA((sum(counts),))],
        cost_estimate=pl.CostEstimate(flops=int(1e6), bytes_accessed=5 << 20, transcendentals=0),
        name="merge",
    )(col_pair, *used, *where, *[piece for pieces in payloads for piece in pieces])


BESIDE = ((2, 6), (1, 4, 7), (3, 5))
LAST = ((3, 4, 5), (1, 7, 2, 6))
PLANS = ((BESIDE, ()), (LAST, (1, 7)))
CODE_BITS = 6


def turn(x, shift, dev_count):
    return lax.ppermute(x, "dev", [(i, (i + shift) % dev_count) for i in range(dev_count)])


def unwritten(shapes):
    return pl.pallas_call(
        lambda *refs: None,
        out_shape=[jax.ShapeDtypeStruct(shape, jnp.float32) for shape in shapes],
        out_specs=[ANY] * len(shapes),
        cost_estimate=pl.CostEstimate(flops=0, bytes_accessed=0, transcendentals=0),
        name="unwritten",
    )()


def exchange_set(shifts, whole, units, choice, dev_count):
    operands = [units[n] for shift in shifts for n in (shift, dev_count - 1 + shift)]

    levels = [(0, 2) if shift in whole else (0, 1, 2) for shift in shifts]
    codes = [code[::-1] for code in itertools.product(*levels[::-1])]

    def branch(used):
        sent = [(u == 2, u == 1) for u in used]
        sent = [flag for pair in sent for flag in pair]

        def run(*arrays):
            rest = list(unwritten([x.shape for x, flag in zip(arrays, sent) if not flag]))
            got = []
            for n, (array, flag) in enumerate(zip(arrays, sent)):
                got.append(turn(array, shifts[n // 2], dev_count) if flag else rest.pop(0))
            return got

        return run

    return lax.switch(choice, [branch(code) for code in codes], *operands)


def exchange_all(blocks, capacity, dev_count):
    me = lax.axis_index("dev")
    ids = jnp.arange(dev_count * capacity, dtype=jnp.int32)
    away, place = ids // capacity, ids % capacity
    send = jnp.take(blocks, (away - me) % dev_count * capacity + place, axis=0)
    got = lax.all_to_all(send, "dev", split_axis=0, concat_axis=0, tiled=True)
    return jnp.take(got, (me - away) % dev_count * capacity + place, axis=0)


def ordered(first, then):
    first, then = lax.optimization_barrier((first, then))
    return first, then


def body(adjacency, features, col_slot, row_slot, row_pair, col_pair, col_offset):
    dev_count = lax.axis_size("dev")
    blocks = adjacency.shape[0]
    capacity = 2 * blocks // dev_count
    in_sets = dev_count == 8
    full, size = (dev_count, capacity) if in_sets else (1, capacity * dev_count)

    (maps_a, maps_b), used, slot, where, choice, source, units_x = head(
        adjacency, features.T, col_slot, row_slot, row_pair, col_offset, 2, dev_count, capacity, in_sets
    )

    def over_grp(x, distance):
        pairs = []
        for g in range(GROUPS):
            for d in range(dev_count):
                to = g ^ (distance if d % 2 == 0 else 3 - distance)
                pairs.append((g * dev_count + d, to * dev_count + d))
        return lax.ppermute(x, ("grp", "dev"), pairs)

    def columns(maps, got1, got2, plan):
        return column_map(maps[1], got1, got2, source, used[plan], slot, full, size)

    got1_a = over_grp(maps_a[0], 1)
    if not in_sets:
        payloads = [[exchange_all(units_x[0], capacity, dev_count)]]
        for maps, got1 in ((maps_a, got1_a), (maps_b, over_grp(maps_b[0], 1))):
            units = columns(maps, got1, over_grp(maps[2] + got1[1], 2), 0)
            payloads.append([exchange_all(units[0], capacity, dev_count)])
        coarse_adjacency, coarse_features = merge(payloads, (0, 0, 0), used, where, col_pair, full)
        return coarse_adjacency, coarse_features.T

    def collect(units, sets, parts):
        pieces = list(units)
        for shifts, part in zip(sets, parts):
            for i, shift in enumerate(shifts):
                pieces[shift], pieces[dev_count - 1 + shift] = part[2 * i], part[2 * i + 1]
        return pieces

    def exchange(units, plan, which):
        sets, whole = PLANS[plan]
        parts = []
        for n in which:
            code = lax.shift_right_logical(choice, jnp.int32(CODE_BITS * (plan * len(BESIDE) + n)))
            code = jnp.bitwise_and(code, 2**CODE_BITS - 1)
            parts.append(exchange_set(sets[n], whole, units, code, dev_count))
        return parts

    part_x = exchange(units_x, 0, (0, 1))
    (part_x, maps_b), got1_a = ordered((part_x, maps_b), got1_a)
    sum_a = maps_a[2] + got1_a[1]
    sum_a, units_x = ordered(sum_a, units_x)
    got2_a = over_grp(sum_a, 2)
    part_x += exchange(units_x, 0, (2,))
    (part_x, maps_b), got2_a = ordered((part_x, maps_b), got2_a)
    got1_b = over_grp(maps_b[0], 1)
    units_a = columns(maps_a, got1_a, got2_a, 0)
    part_a = exchange(units_a, 0, (0, 1))
    part_a, got1_b = ordered(part_a, got1_b)
    sum_b = maps_b[2] + got1_b[1]
    sum_b, units_a = ordered(sum_b, units_a)
    got2_b = over_grp(sum_b, 2)
    part_a += exchange(units_a, 0, (2,))
    part_a, got2_b = ordered(part_a, got2_b)
    units_b = columns(maps_b, got1_b, got2_b, 1)
    part_b = exchange(units_b, 1, (0, 1))

    payloads = [
        collect(units_x, BESIDE, part_x),
        collect(units_a, BESIDE, part_a),
        collect(units_b, LAST, part_b),
    ]
    coarse_adjacency, coarse_features = merge(payloads, (0, 0, 1), used, where, col_pair, full)
    return coarse_adjacency, coarse_features.T


def solution(mesh):
    in_specs = (
        P("dev", "grp", None),
        P("dev", "grp"),
        P("dev", None),
        P("grp", None),
        P(),
        P(),
        P(),
    )
    out_specs = (P("dev", "grp", None), P("dev", "grp"))
    return jax.shard_map(body, mesh=mesh, in_specs=in_specs, out_specs=out_specs, check_vma=False)
```
